32 devices in a mesh: ct: 4 (over y, x), tile: 8 (over z, core).
Axes of the slice: x: 2, y: 2, z: 4, core: 2. Of those that a mesh axis runs over, the one named last changes fastest.
Arguments:
- voltages: int32 [8, 256, 2048], P('tile', 'ct'), may hold values from -8 to 7
- fir_taps: float32 [4, 1024], replicated, may hold values from -3 to 3
- tile_map: int32 [528, 2], P('tile'), may hold values from 0 to 31, as said below
Outputs:
- visibilities: float32 [528, 1024, 128], P('tile', 'ct')
The draws below stay inside these ranges and needn't reach their ends.
Inputs may be any that keep to these rules, and one draw needn't show every extreme that they name: `tile_map`: each row holds two block numbers, the first not above the second; every such pair of the 32 blocks stands in exactly one row.
All inputs are finite; a program needn't handle non-finite values.
Results may differ from the reference program's by a relative error of at most 0.0056.
Values may be sent and summed in bfloat16 or wider, within the bound.
A program may use at most 448 MiB of HBM per device.

```python
import math
import jax
import jax.numpy as jnp
import numpy as np
from jax import lax

NCHAN = 1024
INPUTS = 256
TAPS = 4
B = 8
TIME = 8
NB = 32
TILES = 528


def draw_tile_map(key, part):
    block_pairs = np.array([(first, second) for first in range(NB) for second in range(first, NB)], dtype=np.int32)
    shuffled = jax.random.permutation(key, TILES)
    return jnp.asarray(block_pairs)[shuffled]


def plant(values, rng, least, high):
    longest = values.shape.index(max(values.shape))
    spots = []
    for shift in (0, 1):
        where = [jax.random.randint(jax.random.fold_in(rng, axis), (), 0, length) for axis, length in enumerate(values.shape)]
        where[longest] = (where[longest] + shift) % values.shape[longest]
        spots.append(tuple(where))
    return values.at[spots[0]].set(least).at[spots[1]].set(high)


def noise(rng, shape, scale, limit, kind=jnp.bfloat16):
    values = jax.random.normal(rng, shape, jnp.float32) * scale
    return jnp.minimum(jnp.maximum(values, -limit), limit).astype(kind)


def setup_inputs(seed: int = 0) -> dict:
    keys = jax.random.split(jax.random.key(seed), 4)
    return {
        "voltages": plant(jax.random.randint(keys[0], (TIME, INPUTS, 2 * NCHAN), -8, 8), jax.random.fold_in(keys[0], 1), -8, 7).astype(jnp.int32),
        "fir_taps": noise(keys[1], (TAPS, NCHAN), TAPS ** -0.5, 3.0, jnp.float32),
        "tile_map": draw_tile_map(jax.random.fold_in(keys[3], 71), 0),
    }


def dft_table(channels):
    positions = jnp.arange(channels, dtype=jnp.int32)
    products = positions[:, None] * positions[None, :] % channels
    angles = products.astype(jnp.float32) * (2.0 * math.pi / channels)
    norm_scale = 1.0 / math.sqrt(channels)
    cosine = jnp.cos(angles) * norm_scale
    sine = jnp.sin(angles) * norm_scale
    upper_half = jnp.concatenate([cosine, -sine], axis=1)
    lower_half = jnp.concatenate([sine, cosine], axis=1)
    return jnp.concatenate([upper_half, lower_half], axis=0).astype(jnp.bfloat16)

def reference(voltages, fir_taps, tile_map):
    samples = voltages.astype(jnp.float32) * 0.25
    tap_gains = jnp.concatenate([fir_taps, fir_taps], axis=1)
    filtered = jnp.zeros(samples.shape, jnp.float32)
    for tap_index in range(TAPS):
        delayed = jnp.pad(samples[:TIME - tap_index], ((tap_index, 0), (0, 0), (0, 0)))
        filtered = filtered + tap_gains[tap_index][None, None, :] * delayed
    filtered = filtered.astype(jnp.bfloat16)
    spectra = jnp.dot(filtered.reshape(TIME * INPUTS, 2 * NCHAN), dft_table(NCHAN), preferred_element_type=jnp.float32).astype(jnp.bfloat16)
    blocks = spectra.reshape(TIME, NB, B, 2, NCHAN).astype(jnp.float32)

    def one_tile(block_pair):
        left_side = lax.dynamic_index_in_dim(blocks, block_pair[0], axis=1, keepdims=False)
        right_side = lax.dynamic_index_in_dim(blocks, block_pair[1], axis=1, keepdims=False)
        swapped = jnp.stack([left_side[:, :, 1], -left_side[:, :, 0]], axis=2)
        stacked = jnp.stack([left_side, swapped], axis=0)
        sums = jnp.einsum('qtapc,tbpc->cqab', stacked, right_side, precision=lax.Precision.HIGHEST)
        return sums.reshape(NCHAN, 2 * B * B) / TIME
    return lax.map(one_tile, tile_map)
```

```python
import functools
import math

import jax
import jax.numpy as jnp
import ml_dtypes
import numpy as np
from jax import lax
from jax.experimental import pallas as pl
from jax.experimental.pallas import tpu as pltpu
from jax.sharding import PartitionSpec as P

B = 8


def half_table(channels):
    positions = np.arange(channels, dtype=np.int64)
    products = positions[:, None] * positions[None, :] % channels
    step = np.float32(2.0 * math.pi / channels)
    angles = (products.astype(np.float32) * step).astype(np.float64)
    both = np.concatenate([np.cos(angles), np.sin(angles)], axis=1) / math.sqrt(channels)
    return both.astype(np.float32).astype(ml_dtypes.bfloat16)


def earlier_frames(volts, needed):
    frames = volts.shape[0]
    count = lax.axis_size("tile")
    parts = []
    for hop in range(1, -(-needed // frames) + 1):
        rows = min(frames, needed - (hop - 1) * frames)
        pairs = [(source, source + hop) for source in range(count - hop)]
        parts.insert(0, lax.ppermute(volts[frames - rows:], "tile", pairs))
    return parts


def correlate_kernel(group, scale, pairs_ref, g_ref, out_ref, wide):
    tiles, shards, frames, _, in_dev, span = g_ref.shape
    per_src = in_dev // B
    total = tiles * frames
    lanes = min(span, 128)

    @pl.when(pl.program_id(0) == 0)
    def _():
        def widen(index, carry):
            tile, src = index // shards, index % shards
            for frame in range(frames):
                for part in range(2):
                    slab = g_ref[tile, src, frame, part].astype(jnp.float32)
                    for blk in range(per_src):
                        wide[src * per_src + blk, (tile * frames + frame) * 2 + part] = slab[blk * B:(blk + 1) * B]
            return carry
        lax.fori_loop(0, tiles * shards, widen, 0)

    def one_tile(index, carry):
        row = pl.program_id(0) * group + index
        first, second = pairs_ref[row, 0], pairs_ref[row, 1]
        for chunk in range(span // lanes):
            cols = pl.ds(chunk * lanes, lanes)

            def add_frame(t, sums):
                sums = list(sums)
                right_re = wide[second, 2 * t, :, cols]
                right_im = wide[second, 2 * t + 1, :, cols]
                for a in range(B):
                    left_re = jnp.broadcast_to(wide[first, 2 * t, pl.ds(a, 1), cols], (B, lanes))
                    left_im = jnp.broadcast_to(wide[first, 2 * t + 1, pl.ds(a, 1), cols], (B, lanes))
                    sums[a] = sums[a] + (left_re * right_re + left_im * right_im)
                    sums[B + a] = sums[B + a] + (left_im * right_re - left_re * right_im)
                return tuple(sums)

            sums = tuple(jnp.zeros((B, lanes), jnp.float32) for _ in range(2 * B))
            if total <= 8:
                for t in range(total):
                    sums = add_frame(t, sums)
            else:
                sums = lax.fori_loop(0, total, add_frame, sums)
            rows = jnp.concatenate(sums, axis=0) * scale
            out_ref[index, cols, :] = rows.T
        return carry
    lax.fori_loop(0, group, one_tile, 0)


def correlate(gathered, pairs):
    tiles, shards, frames, _, in_dev, span = gathered.shape
    rows = pairs.shape[0]
    total = tiles * frames
    group = max(size for size in range(1, 12) if rows % size == 0)
    return pl.pallas_call(
        functools.partial(correlate_kernel, group, 1.0 / total),
        grid_spec=pltpu.PrefetchScalarGridSpec(
            num_scalar_prefetch=1,
            grid=(rows // group,),
            in_specs=[pl.BlockSpec(gathered.shape, lambda i, pairs: (0,) * 6)],
            out_specs=pl.BlockSpec((group, span, 2 * B * B), lambda i, pairs: (i, 0, 0)),
            scratch_shapes=[pltpu.VMEM((shards * in_dev // B, 2 * total, B, span), jnp.float32)],
        ),
        out_shape=jax.ShapeDtypeStruct((rows, span, 2 * B * B), jnp.float32),
        compiler_params=pltpu.CompilerParams(vmem_limit_bytes=48 * 2**20),
        cost_estimate=pl.CostEstimate(
            flops=rows * span * 2 * B * B * 4 * total,
            bytes_accessed=rows * span * 2 * B * B * 4,
            transcendentals=0,
        ),
        name="correlate",
    )(pairs, gathered)


def per_device(voltages, fir_taps, tile_map):
    frames, in_dev, row_width = voltages.shape
    channels = row_width // 2
    taps = fir_taps.shape[0]
    shards = lax.axis_size("ct")
    span = channels // shards
    volts = voltages.astype(jnp.bfloat16)
    history = jnp.concatenate(earlier_frames(volts, taps - 1) + [volts], axis=0)
    history = history.astype(jnp.float32) * 0.25
    gains = jnp.concatenate([fir_taps, fir_taps], axis=1)
    filtered = jnp.zeros((frames, in_dev, row_width), jnp.float32)
    for tap in range(taps):
        start = taps - 1 - tap
        filtered = filtered + gains[tap][None, None, :] * history[start:start + frames]
    filtered = filtered.astype(jnp.bfloat16)
    halves = jnp.stack([filtered[..., :channels], filtered[..., channels:]], axis=1)
    products = jnp.dot(
        halves.reshape(frames * 2 * in_dev, channels),
        jnp.asarray(half_table(channels)),
        preferred_element_type=jnp.float32,
    ).reshape(frames, 2, in_dev, 2, shards, span)
    real = products[:, 0, :, 0] + products[:, 1, :, 1]
    imag = products[:, 1, :, 0] - products[:, 0, :, 1]
    spectra = jnp.stack([real, imag], axis=1).astype(jnp.bfloat16)
    spectra = spectra.transpose(3, 0, 1, 2, 4)
    turned = lax.all_to_all(spectra, "ct", split_axis=0, concat_axis=0, tiled=True)
    gathered = lax.all_gather(turned, "tile", axis=0, tiled=False)
    return correlate(gathered, tile_map)


def solution(mesh):
    in_specs = (P("tile", "ct", None), P(), P("tile", None))
    out_specs = P("tile", "ct", None)
    return jax.shard_map(
        per_device, mesh=mesh, in_specs=in_specs, out_specs=out_specs, check_vma=False
    )
```

```python
import functools
import math

import jax
import jax.numpy as jnp
import ml_dtypes
import numpy as np
from jax import lax
from jax.experimental import pallas as pl
from jax.experimental.pallas import tpu as pltpu
from jax.sharding import PartitionSpec as P

B = 8
MESH = pl.DeviceIdType.MESH


def half_table(channels):
    positions = np.arange(channels, dtype=np.int64)
    products = positions[:, None] * positions[None, :] % channels
    step = np.float32(2.0 * math.pi / channels)
    angles = (products.astype(np.float32) * step).astype(np.float64)
    both = np.concatenate([np.cos(angles), np.sin(angles)], axis=1) / math.sqrt(channels)
    return both.astype(np.float32).astype(ml_dtypes.bfloat16)


def earlier_frames(volts, needed):
    frames = volts.shape[0]
    count = lax.axis_size("tile")
    parts = []
    for hop in range(1, -(-needed // frames) + 1):
        rows = min(frames, needed - (hop - 1) * frames)
        pairs = [(source, source + hop) for source in range(count - hop)]
        parts.insert(0, lax.ppermute(volts[frames - rows:], "tile", pairs))
    return parts


def correlate_kernel(group, scale, pairs_ref, g_ref, out_ref, wide):
    blocks, rows, span = g_ref.shape
    total = rows // (2 * B)
    lanes = min(span, 128)

    @pl.when(pl.program_id(0) == 0)
    def _():
        def widen(block, carry):
            wide[block] = g_ref[block].astype(jnp.float32).reshape(2 * total, B, span)
            return carry
        lax.fori_loop(0, blocks, widen, 0)

    def one_tile(index, carry):
        row = pl.program_id(0) * group + index
        first, second = pairs_ref[row, 0], pairs_ref[row, 1]
        for chunk in range(span // lanes):
            cols = pl.ds(chunk * lanes, lanes)

            def add_frame(t, sums):
                sums = list(sums)
                right_re = wide[second, 2 * t, :, cols]
                right_im = wide[second, 2 * t + 1, :, cols]
                for a in range(B):
                    left_re = jnp.broadcast_to(wide[first, 2 * t, pl.ds(a, 1), cols], (B, lanes))
                    left_im = jnp.broadcast_to(wide[first, 2 * t + 1, pl.ds(a, 1), cols], (B, lanes))
                    sums[a] = sums[a] + (left_re * right_re + left_im * right_im)
                    sums[B + a] = sums[B + a] + (left_im * right_re - left_re * right_im)
                return tuple(sums)

            sums = tuple(jnp.zeros((B, lanes), jnp.float32) for _ in range(2 * B))
            if total <= 8:
                for t in range(total):
                    sums = add_frame(t, sums)
            else:
                sums = lax.fori_loop(0, total, add_frame, sums)
            rows = jnp.concatenate(sums, axis=0) * scale
            out_ref[index, cols, :] = rows.T
        return carry
    lax.fori_loop(0, group, one_tile, 0)


def correlate(gathered, pairs):
    blocks, depth, span = gathered.shape
    total = depth // (2 * B)
    rows = pairs.shape[0]
    group = max(size for size in range(1, 12) if rows % size == 0)
    return pl.pallas_call(
        functools.partial(correlate_kernel, group, 1.0 / total),
        grid_spec=pltpu.PrefetchScalarGridSpec(
            num_scalar_prefetch=1,
            grid=(rows // group,),
            in_specs=[pl.BlockSpec(gathered.shape, lambda i, pairs: (0, 0, 0))],
            out_specs=pl.BlockSpec((group, span, 2 * B * B), lambda i, pairs: (i, 0, 0)),
            scratch_shapes=[pltpu.VMEM((blocks, 2 * total, B, span), jnp.float32)],
        ),
        out_shape=jax.ShapeDtypeStruct((rows, span, 2 * B * B), jnp.float32),
        compiler_params=pltpu.CompilerParams(vmem_limit_bytes=48 * 2**20),
        cost_estimate=pl.CostEstimate(
            flops=rows * span * 2 * B * B * 4 * total,
            bytes_accessed=rows * span * 2 * B * B * 4,
            transcendentals=0,
        ),
        name="correlate",
    )(pairs, gathered)


def front_kernel(volts_ref, gains_ref, table_hbm, buf, table, outbox, inbox, half, spec,
                 table_sem, turn_send, turn_recv, ct_send, ct_recv,
                 up_send, up_recv, down_send, down_recv, core_send, core_recv):
    shards, tiles = lax.axis_size("ct"), lax.axis_size("tile")
    levels = tiles // 2
    taps, channels = gains_ref.shape
    span = channels // shards
    c, t = lax.axis_index("ct"), lax.axis_index("tile")
    z, k = t // 2, t % 2

    fetch = pltpu.make_async_copy(table_hbm, table, table_sem)
    fetch.start()
    barrier = pltpu.get_barrier_semaphore()
    for off in range(1, tiles):
        pl.semaphore_signal(barrier, inc=1, device_id={"tile": lax.rem(t + off, tiles)}, device_id_type=MESH)
    for off in range(1, shards):
        pl.semaphore_signal(barrier, inc=1, device_id={"ct": lax.rem(c + off, shards)}, device_id_type=MESH)
    for dest in range(tiles):
        part = volts_ref[dest * B:(dest + 1) * B].astype(jnp.float32)
        outbox[dest] = jnp.concatenate([part[:, :channels], part[:, channels:]], axis=0).astype(jnp.bfloat16)
    pl.semaphore_wait(barrier, tiles + shards - 2)

    def turn(off, slot):
        dest = lax.rem(t + off, tiles)
        return pltpu.make_async_remote_copy(
            src_ref=outbox.at[dest], dst_ref=inbox.at[slot],
            send_sem=turn_send.at[off], recv_sem=turn_recv.at[off],
            device_id={"tile": dest}, device_id_type=MESH)

    for off in range(1, tiles):
        turn(off, t).start()
    inbox[t] = outbox[t]
    for off in range(1, tiles):
        turn(off, lax.rem(t - off + tiles, tiles)).wait_recv()

    for frame in range(tiles):
        total = jnp.zeros((2 * B, channels), jnp.float32)
        for tap in range(min(taps, frame + 1)):
            samples = inbox[frame - tap].astype(jnp.float32) * 0.25
            total = total + gains_ref[tap:tap + 1, :] * samples
        half[frame * 2 * B:(frame + 1) * 2 * B] = total.astype(jnp.bfloat16)
    fetch.wait()

    def ct_copy(off, block):
        dest = lax.rem(c + off, shards)
        return pltpu.make_async_remote_copy(
            src_ref=spec.at[dest], dst_ref=buf.at[block, t],
            send_sem=ct_send.at[off], recv_sem=ct_recv.at[off],
            device_id={"ct": dest}, device_id_type=MESH)

    def piece(slab, j, send, recv, dest):
        place = buf.at[lax.rem(c - j + shards, shards), slab]
        return pltpu.make_async_remote_copy(
            src_ref=place, dst_ref=place, send_sem=send, recv_sem=recv,
            device_id={"tile": dest}, device_id_type=MESH)

    def up(d, j):
        return piece(t - 2 * d, j, up_send.at[d, j], up_recv.at[d, j], t + 2)

    def up_arrival(d, j):
        return piece(t - 2 * d, j, up_send.at[d - 1, j], up_recv.at[d - 1, j], t + 2)

    def down(d, j):
        return piece(t + 2 * d, j, down_send.at[d, j], down_recv.at[d, j], t - 2)

    def down_arrival(d, j):
        return piece(t + 2 * d, j, down_send.at[d - 1, j], down_recv.at[d - 1, j], t - 2)

    def core(step, j, other):
        slab = t + 2 * step + (1 - 2 * k if other else 0)
        return piece(slab, j, core_send.at[levels - 1 + step, j], core_recv.at[levels - 1 + step, j], t + 1 - 2 * k)

    def send_own(j):
        @pl.when(z + 1 < levels)
        def _():
            up(0, j).start()

        @pl.when(z >= 1)
        def _():
            down(0, j).start()
        core(0, j, False).start()

    for off in range(shards):
        dest = lax.rem(c + off, shards)
        product = jnp.dot(half[...], table[dest], preferred_element_type=jnp.float32)
        product = product.reshape(tiles, 2, B, 2 * span)
        real = product[:, 0, :, :span] + product[:, 1, :, span:]
        imag = product[:, 1, :, :span] - product[:, 0, :, span:]
        rows = jnp.concatenate([real[:, None], imag[:, None]], axis=1).reshape(tiles * 2 * B, span)
        if off == 0:
            buf[c, t] = rows.astype(jnp.bfloat16)
            send_own(0)
        else:
            spec[dest] = rows.astype(jnp.bfloat16)
            ct_copy(off, c).start()
    for off in range(1, shards):
        ct_copy(off, lax.rem(c - off + shards, shards)).wait_recv()
        send_own(off)

    for d in range(1, levels):
        def pass_on(j, carry, d=d):
            @pl.when(z >= d)
            def _():
                up_arrival(d, j).wait_recv()

                @pl.when(z + 1 < levels)
                def _():
                    up(d, j).start()
                core(-d, j, False).start()

            @pl.when(z + d < levels)
            def _():
                down_arrival(d, j).wait_recv()

                @pl.when(z >= 1)
                def _():
                    down(d, j).start()
                core(d, j, False).start()
            return carry
        lax.fori_loop(0, shards, pass_on, 0)

    for off in range(1, tiles):
        turn(off, t).wait_send()
    for off in range(1, shards):
        ct_copy(off, c).wait_send()
    for d in range(levels):
        def finish(j, carry, d=d):
            @pl.when((z >= d) & (z + 1 < levels))
            def _():
                up(d, j).wait_send()

            @pl.when((z + d < levels) & (z >= 1))
            def _():
                down(d, j).wait_send()

            @pl.when(z >= d)
            def _():
                core(-d, j, False).wait_send()
                core(-d, j, True).wait_recv()
            if d > 0:
                @pl.when(z + d < levels)
                def _():
                    core(d, j, False).wait_send()
                    core(d, j, True).wait_recv()
            return carry
        lax.fori_loop(0, shards, finish, 0)


def front(voltages, fir_taps):
    shards, tiles = lax.axis_size("ct"), lax.axis_size("tile")
    _, in_dev, row_width = voltages.shape
    channels = row_width // 2
    span = channels // shards
    levels = tiles // 2
    table = half_table(channels).reshape(channels, 2, shards, span).transpose(2, 0, 1, 3)
    table = np.ascontiguousarray(table.reshape(shards, channels, 2 * span))
    depth = tiles * 2 * B
    vmem = pl.BlockSpec(memory_space=pltpu.VMEM)
    dma = pltpu.SemaphoreType.DMA
    gathered = pl.pallas_call(
        front_kernel,
        in_specs=[vmem, vmem, pl.BlockSpec(memory_space=pl.ANY)],
        out_specs=vmem,
        out_shape=jax.ShapeDtypeStruct((shards, tiles, depth, span), jnp.bfloat16),
        scratch_shapes=[
            pltpu.VMEM(table.shape, jnp.bfloat16),
            pltpu.VMEM((tiles, 2 * B, channels), jnp.bfloat16),
            pltpu.VMEM((tiles, 2 * B, channels), jnp.bfloat16),
            pltpu.VMEM((depth, channels), jnp.bfloat16),
            pltpu.VMEM((shards, depth, span), jnp.bfloat16),
            dma, dma((tiles,)), dma((tiles,)), dma((shards,)), dma((shards,)),
            dma((levels, shards)), dma((levels, shards)), dma((levels, shards)), dma((levels, shards)),
            dma((2 * levels - 1, shards)), dma((2 * levels - 1, shards)),
        ],
        compiler_params=pltpu.CompilerParams(
            collective_id=0, has_side_effects=True, vmem_limit_bytes=48 * 2**20),
        cost_estimate=pl.CostEstimate(
            flops=depth * channels * 4 * channels, bytes_accessed=4 * channels * channels, transcendentals=0),
        name="front",
    )(voltages[0], fir_taps, jnp.asarray(table))
    return gathered.reshape(shards * tiles, depth, span)


def front_by_collectives(voltages, fir_taps):
    frames, in_dev, row_width = voltages.shape
    channels = row_width // 2
    taps = fir_taps.shape[0]
    shards = lax.axis_size("ct")
    span = channels // shards
    volts = voltages.astype(jnp.bfloat16)
    history = jnp.concatenate(earlier_frames(volts, taps - 1) + [volts], axis=0)
    history = history.astype(jnp.float32) * 0.25
    gains = jnp.concatenate([fir_taps, fir_taps], axis=1)
    filtered = jnp.zeros((frames, in_dev, row_width), jnp.float32)
    for tap in range(taps):
        start = taps - 1 - tap
        filtered = filtered + gains[tap][None, None, :] * history[start:start + frames]
    filtered = filtered.astype(jnp.bfloat16)
    halves = jnp.stack([filtered[..., :channels], filtered[..., channels:]], axis=1)
    products = jnp.dot(
        halves.reshape(frames * 2 * in_dev, channels),
        jnp.asarray(half_table(channels)),
        preferred_element_type=jnp.float32,
    ).reshape(frames, 2, in_dev, 2, shards, span)
    real = products[:, 0, :, 0] + products[:, 1, :, 1]
    imag = products[:, 1, :, 0] - products[:, 0, :, 1]
    spectra = jnp.stack([real, imag], axis=1).astype(jnp.bfloat16)
    spectra = spectra.transpose(3, 0, 1, 2, 4)
    turned = lax.all_to_all(spectra, "ct", split_axis=0, concat_axis=0, tiled=True)
    gathered = lax.all_gather(turned, "tile", axis=0, tiled=False)
    tiles = gathered.shape[0]
    gathered = gathered.reshape(tiles, shards, frames, 2, in_dev // B, B, span).transpose(1, 4, 0, 2, 3, 5, 6)
    return gathered.reshape(shards * in_dev // B, tiles * frames * 2 * B, span)


def per_device(voltages, fir_taps, tile_map):
    frames, in_dev, _ = voltages.shape
    tiles = lax.axis_size("tile")
    one_block_each = frames == 1 and in_dev == tiles * B and tiles % 2 == 0
    make = front if one_block_each else front_by_collectives
    return correlate(make(voltages, fir_taps), tile_map)


def solution(mesh):
    in_specs = (P("tile", "ct", None), P(), P("tile", None))
    out_specs = P("tile", "ct", None)
    return jax.shard_map(
        per_device, mesh=mesh, in_specs=in_specs, out_specs=out_specs, check_vma=False
    )
```

```python
import functools
import math

import jax
import jax.numpy as jnp
import ml_dtypes
import numpy as np
from jax import lax
from jax.experimental import pallas as pl
from jax.experimental.pallas import tpu as pltpu
from jax.sharding import PartitionSpec as P

B = 8
MESH = pl.DeviceIdType.MESH


def half_table(channels):
    positions = np.arange(channels, dtype=np.int64)
    products = positions[:, None] * positions[None, :] % channels
    step = np.float32(2.0 * math.pi / channels)
    angles = (products.astype(np.float32) * step).astype(np.float64)
    both = np.concatenate([np.cos(angles), np.sin(angles)], axis=1) / math.sqrt(channels)
    return both.astype(np.float32).astype(ml_dtypes.bfloat16)


def earlier_frames(volts, needed):
    frames = volts.shape[0]
    count = lax.axis_size("tile")
    parts = []
    for hop in range(1, -(-needed // frames) + 1):
        rows = min(frames, needed - (hop - 1) * frames)
        pairs = [(source, source + hop) for source in range(count - hop)]
        parts.insert(0, lax.ppermute(volts[frames - rows:], "tile", pairs))
    return parts


def correlate_kernel(group, scale, pairs_ref, g_ref, out_ref, wide):
    blocks, rows, span = g_ref.shape
    total = rows // (2 * B)
    lanes = min(span, 128)

    @pl.when(pl.program_id(0) == 0)
    def _():
        def widen(block, carry):
            both = g_ref[block].astype(jnp.float32).reshape(total, 2, B, span)
            real, imag = both[:, 0], both[:, 1]
            for plane, value in enumerate((real, imag, real + imag, real - imag)):
                wide[block, plane] = value
            return carry
        lax.fori_loop(0, blocks, widen, 0)

    def one_tile(index, carry):
        row = pl.program_id(0) * group + index
        first, second = pairs_ref[row, 0], pairs_ref[row, 1]
        for chunk in range(span // lanes):
            cols = pl.ds(chunk * lanes, lanes)

            def add_frame(t, sums):
                sums = list(sums)
                right_re = wide[second, 0, t, :, cols]
                right_sum = wide[second, 2, t, :, cols]
                right_diff = wide[second, 3, t, :, cols]
                for a in range(B):
                    left_re, left_im, left_sum = (
                        jnp.broadcast_to(wide[first, plane, t, pl.ds(a, 1), cols], (B, lanes))
                        for plane in range(3))
                    sums[a] = sums[a] + left_sum * right_re
                    sums[B + a] = sums[B + a] + left_re * right_sum
                    sums[2 * B + a] = sums[2 * B + a] + left_im * right_diff
                return tuple(sums)

            sums = tuple(jnp.zeros((B, lanes), jnp.float32) for _ in range(3 * B))
            if total <= 8:
                for t in range(total):
                    sums = add_frame(t, sums)
            else:
                sums = lax.fori_loop(0, total, add_frame, sums)
            sums = [sums[a] - sums[2 * B + a] for a in range(B)] + [sums[a] - sums[B + a] for a in range(B)]
            rows = jnp.concatenate(sums, axis=0) * scale
            out_ref[index, cols, :] = rows.T
        return carry
    lax.fori_loop(0, group, one_tile, 0)


def correlate(gathered, pairs):
    blocks, depth, span = gathered.shape
    total = depth // (2 * B)
    rows = pairs.shape[0]
    group = max(size for size in range(1, 12) if rows % size == 0)
    return pl.pallas_call(
        functools.partial(correlate_kernel, group, 1.0 / total),
        grid_spec=pltpu.PrefetchScalarGridSpec(
            num_scalar_prefetch=1,
            grid=(rows // group,),
            in_specs=[pl.BlockSpec(gathered.shape, lambda i, pairs: (0, 0, 0))],
            out_specs=pl.BlockSpec((group, span, 2 * B * B), lambda i, pairs: (i, 0, 0)),
            scratch_shapes=[pltpu.VMEM((blocks, 4, total, B, span), jnp.float32)],
        ),
        out_shape=jax.ShapeDtypeStruct((rows, span, 2 * B * B), jnp.float32),
        compiler_params=pltpu.CompilerParams(vmem_limit_bytes=48 * 2**20),
        cost_estimate=pl.CostEstimate(
            flops=rows * span * 2 * B * B * 4 * total,
            bytes_accessed=rows * span * 2 * B * B * 4,
            transcendentals=0,
        ),
        name="correlate",
    )(pairs, gathered)


def front_kernel(volts_hbm, gains_hbm, table_hbm, buf, volts_ref, gains_ref, table, outbox, inbox, half, spec,
                 fetch_sem, turn_send, turn_recv, ct_send, ct_recv,
                 up_send, up_recv, down_send, down_recv, core_send, core_recv):
    shards, tiles = lax.axis_size("ct"), lax.axis_size("tile")
    levels = tiles // 2
    taps, channels = gains_hbm.shape
    span = channels // shards
    c, t = lax.axis_index("ct"), lax.axis_index("tile")
    z, k = t // 2, t % 2

    fetch_volts = pltpu.make_async_copy(volts_hbm, volts_ref, fetch_sem.at[0])
    fetch_gains = pltpu.make_async_copy(gains_hbm, gains_ref, fetch_sem.at[1])
    fetch_table = pltpu.make_async_copy(table_hbm, table, fetch_sem.at[2])
    for fetch in (fetch_volts, fetch_gains, fetch_table):
        fetch.start()
    barrier = pltpu.get_barrier_semaphore()
    for off in range(1, tiles):
        pl.semaphore_signal(barrier, inc=1, device_id={"tile": lax.rem(t + off, tiles)}, device_id_type=MESH)
    for off in range(1, shards):
        pl.semaphore_signal(barrier, inc=1, device_id={"ct": lax.rem(c + off, shards)}, device_id_type=MESH)
    fetch_volts.wait()
    for dest in range(tiles):
        part = volts_ref[dest * B:(dest + 1) * B].astype(jnp.float32)
        outbox[dest] = jnp.concatenate([part[:, :channels], part[:, channels:]], axis=0).astype(jnp.bfloat16)
    pl.semaphore_wait(barrier, tiles + shards - 2)

    def turn(off, slot):
        dest = lax.rem(t + off, tiles)
        return pltpu.make_async_remote_copy(
            src_ref=outbox.at[dest], dst_ref=inbox.at[slot],
            send_sem=turn_send.at[off], recv_sem=turn_recv.at[off],
            device_id={"tile": dest}, device_id_type=MESH)

    by_distance = sorted(range(1, tiles), key=lambda off: -min(off, tiles - off))
    for off in by_distance:
        turn(off, t).start()
    inbox[t] = outbox[t]
    for off in range(1, tiles):
        turn(off, lax.rem(t - off + tiles, tiles)).wait_recv()

    fetch_gains.wait()
    for frame in range(tiles):
        total = jnp.zeros((2 * B, channels), jnp.float32)
        for tap in range(min(taps, frame + 1)):
            samples = inbox[frame - tap].astype(jnp.float32) * 0.25
            total = total + gains_ref[tap:tap + 1, :] * samples
        half[frame * 2 * B:(frame + 1) * 2 * B] = total.astype(jnp.bfloat16)
    fetch_table.wait()

    def ct_copy(off, block):
        dest = lax.rem(c + off, shards)
        return pltpu.make_async_remote_copy(
            src_ref=spec.at[dest], dst_ref=buf.at[block, t],
            send_sem=ct_send.at[off], recv_sem=ct_recv.at[off],
            device_id={"ct": dest}, device_id_type=MESH)

    def piece(slab, j, send, recv, dest):
        place = buf.at[lax.rem(c - j + shards, shards), slab]
        return pltpu.make_async_remote_copy(
            src_ref=place, dst_ref=place, send_sem=send, recv_sem=recv,
            device_id={"tile": dest}, device_id_type=MESH)

    def up(d, j):
        return piece(t - 2 * d, j, up_send.at[d, j], up_recv.at[d, j], t + 2)

    def up_arrival(d, j):
        return piece(t - 2 * d, j, up_send.at[d - 1, j], up_recv.at[d - 1, j], t + 2)

    def down(d, j):
        return piece(t + 2 * d, j, down_send.at[d, j], down_recv.at[d, j], t - 2)

    def down_arrival(d, j):
        return piece(t + 2 * d, j, down_send.at[d - 1, j], down_recv.at[d - 1, j], t - 2)

    def core(step, j, other):
        slab = t + 2 * step + (1 - 2 * k if other else 0)
        return piece(slab, j, core_send.at[levels - 1 + step, j], core_recv.at[levels - 1 + step, j], t + 1 - 2 * k)

    def send_own(j):
        @pl.when(z + 1 < levels)
        def _():
            up(0, j).start()

        @pl.when(z >= 1)
        def _():
            down(0, j).start()
        core(0, j, False).start()

    for off in range(shards):
        dest = lax.rem(c + off, shards)
        product = jnp.dot(half[...], table[dest], preferred_element_type=jnp.float32)
        product = product.reshape(tiles, 2, B, 2 * span)
        real = product[:, 0, :, :span] + product[:, 1, :, span:]
        imag = product[:, 1, :, :span] - product[:, 0, :, span:]
        rows = jnp.concatenate([real[:, None], imag[:, None]], axis=1).reshape(tiles * 2 * B, span)
        if off == 0:
            buf[c, t] = rows.astype(jnp.bfloat16)
            send_own(0)
        else:
            spec[dest] = rows.astype(jnp.bfloat16)
            ct_copy(off, c).start()
    for off in range(1, shards):
        ct_copy(off, lax.rem(c - off + shards, shards)).wait_recv()
        send_own(off)

    for d in range(1, levels):
        def pass_on(j, carry, d=d):
            @pl.when(z >= d)
            def _():
                up_arrival(d, j).wait_recv()

                @pl.when(z + 1 < levels)
                def _():
                    up(d, j).start()
                core(-d, j, False).start()

            @pl.when(z + d < levels)
            def _():
                down_arrival(d, j).wait_recv()

                @pl.when(z >= 1)
                def _():
                    down(d, j).start()
                core(d, j, False).start()
            return carry
        lax.fori_loop(0, shards, pass_on, 0)

    for off in range(1, tiles):
        turn(off, t).wait_send()
    for off in range(1, shards):
        ct_copy(off, c).wait_send()
    for d in range(levels):
        def finish(j, carry, d=d):
            @pl.when((z >= d) & (z + 1 < levels))
            def _():
                up(d, j).wait_send()

            @pl.when((z + d < levels) & (z >= 1))
            def _():
                down(d, j).wait_send()

            @pl.when(z >= d)
            def _():
                core(-d, j, False).wait_send()
                core(-d, j, True).wait_recv()
            if d > 0:
                @pl.when(z + d < levels)
                def _():
                    core(d, j, False).wait_send()
                    core(d, j, True).wait_recv()
            return carry
        lax.fori_loop(0, shards, finish, 0)


def front(voltages, fir_taps):
    shards, tiles = lax.axis_size("ct"), lax.axis_size("tile")
    _, in_dev, row_width = voltages.shape
    channels = row_width // 2
    span = channels // shards
    levels = tiles // 2
    table = half_table(channels).reshape(channels, 2, shards, span).transpose(2, 0, 1, 3)
    table = np.ascontiguousarray(table.reshape(shards, channels, 2 * span))
    depth = tiles * 2 * B
    vmem = pl.BlockSpec(memory_space=pltpu.VMEM)
    dma = pltpu.SemaphoreType.DMA
    gathered = pl.pallas_call(
        front_kernel,
        in_specs=[pl.BlockSpec(memory_space=pl.ANY)] * 3,
        out_specs=vmem,
        out_shape=jax.ShapeDtypeStruct((shards, tiles, depth, span), jnp.bfloat16),
        scratch_shapes=[
            pltpu.VMEM((in_dev, row_width), jnp.int32),
            pltpu.VMEM(fir_taps.shape, jnp.float32),
            pltpu.VMEM(table.shape, jnp.bfloat16),
            pltpu.VMEM((tiles, 2 * B, channels), jnp.bfloat16),
            pltpu.VMEM((tiles, 2 * B, channels), jnp.bfloat16),
            pltpu.VMEM((depth, channels), jnp.bfloat16),
            pltpu.VMEM((shards, depth, span), jnp.bfloat16),
            dma((3,)), dma((tiles,)), dma((tiles,)), dma((shards,)), dma((shards,)),
            dma((levels, shards)), dma((levels, shards)), dma((levels, shards)), dma((levels, shards)),
            dma((2 * levels - 1, shards)), dma((2 * levels - 1, shards)),
        ],
        compiler_params=pltpu.CompilerParams(
            collective_id=0, has_side_effects=True, vmem_limit_bytes=48 * 2**20),
        cost_estimate=pl.CostEstimate(
            flops=depth * channels * 4 * channels, bytes_accessed=4 * channels * channels, transcendentals=0),
        name="front",
    )(voltages[0], fir_taps, jnp.asarray(table))
    return gathered.reshape(shards * tiles, depth, span)


def front_by_collectives(voltages, fir_taps):
    frames, in_dev, row_width = voltages.shape
    channels = row_width // 2
    taps = fir_taps.shape[0]
    shards = lax.axis_size("ct")
    span = channels // shards
    volts = voltages.astype(jnp.bfloat16)
    history = jnp.concatenate(earlier_frames(volts, taps - 1) + [volts], axis=0)
    history = history.astype(jnp.float32) * 0.25
    gains = jnp.concatenate([fir_taps, fir_taps], axis=1)
    filtered = jnp.zeros((frames, in_dev, row_width), jnp.float32)
    for tap in range(taps):
        start = taps - 1 - tap
        filtered = filtered + gains[tap][None, None, :] * history[start:start + frames]
    filtered = filtered.astype(jnp.bfloat16)
    halves = jnp.stack([filtered[..., :channels], filtered[..., channels:]], axis=1)
    products = jnp.dot(
        halves.reshape(frames * 2 * in_dev, channels),
        jnp.asarray(half_table(channels)),
        preferred_element_type=jnp.float32,
    ).reshape(frames, 2, in_dev, 2, shards, span)
    real = products[:, 0, :, 0] + products[:, 1, :, 1]
    imag = products[:, 1, :, 0] - products[:, 0, :, 1]
    spectra = jnp.stack([real, imag], axis=1).astype(jnp.bfloat16)
    spectra = spectra.transpose(3, 0, 1, 2, 4)
    turned = lax.all_to_all(spectra, "ct", split_axis=0, concat_axis=0, tiled=True)
    gathered = lax.all_gather(turned, "tile", axis=0, tiled=False)
    tiles = gathered.shape[0]
    gathered = gathered.reshape(tiles, shards, frames, 2, in_dev // B, B, span).transpose(1, 4, 0, 2, 3, 5, 6)
    return gathered.reshape(shards * in_dev // B, tiles * frames * 2 * B, span)


def per_device(voltages, fir_taps, tile_map):
    frames, in_dev, _ = voltages.shape
    tiles = lax.axis_size("tile")
    one_block_each = frames == 1 and in_dev == tiles * B and tiles % 2 == 0
    make = front if one_block_each else front_by_collectives
    return correlate(make(voltages, fir_taps), tile_map)


def solution(mesh):
    in_specs = (P("tile", "ct", None), P(), P("tile", None))
    out_specs = P("tile", "ct", None)
    return jax.shard_map(
        per_device, mesh=mesh, in_specs=in_specs, out_specs=out_specs, check_vma=False
    )
```

```python
import functools
import math

import jax
import jax.numpy as jnp
import ml_dtypes
import numpy as np
from jax import lax
from jax.experimental import pallas as pl
from jax.experimental.pallas import tpu as pltpu
from jax.sharding import PartitionSpec as P

B = 8
MESH = pl.DeviceIdType.MESH


def half_table(channels):
    positions = np.arange(channels, dtype=np.int64)
    products = positions[:, None] * positions[None, :] % channels
    step = np.float32(2.0 * math.pi / channels)
    angles = (products.astype(np.float32) * step).astype(np.float64)
    both = np.concatenate([np.cos(angles), np.sin(angles)], axis=1) / math.sqrt(channels)
    return both.astype(np.float32).astype(ml_dtypes.bfloat16)


def earlier_frames(volts, needed):
    frames = volts.shape[0]
    count = lax.axis_size("tile")
    parts = []
    for hop in range(1, -(-needed // frames) + 1):
        rows = min(frames, needed - (hop - 1) * frames)
        pairs = [(source, source + hop) for source in range(count - hop)]
        parts.insert(0, lax.ppermute(volts[frames - rows:], "tile", pairs))
    return parts


def correlate_kernel(group, scale, pairs_ref, g_ref, out_ref, wide):
    blocks, rows, span = g_ref.shape
    total = rows // (2 * B)
    lanes = min(span, 128)

    @pl.when(pl.program_id(0) == 0)
    def _():
        def widen(block, carry):
            both = g_ref[block].astype(jnp.float32).reshape(total, 2, B, span)
            real, imag = both[:, 0], both[:, 1]
            for plane, value in enumerate((real, imag, real + imag, real - imag)):
                wide[block, plane] = value
            return carry
        lax.fori_loop(0, blocks, widen, 0)

    def one_tile(index, carry):
        row = pl.program_id(0) * group + index
        first, second = pairs_ref[row, 0], pairs_ref[row, 1]
        for chunk in range(span // lanes):
            cols = pl.ds(chunk * lanes, lanes)

            def add_frame(t, sums):
                sums = list(sums)
                right_re = wide[second, 0, t, :, cols]
                right_sum = wide[second, 2, t, :, cols]
                right_diff = wide[second, 3, t, :, cols]
                for a in range(B):
                    left_re, left_im, left_sum = (
                        jnp.broadcast_to(wide[first, plane, t, pl.ds(a, 1), cols], (B, lanes))
                        for plane in range(3))
                    sums[a] = sums[a] + left_sum * right_re
                    sums[B + a] = sums[B + a] + left_re * right_sum
                    sums[2 * B + a] = sums[2 * B + a] + left_im * right_diff
                return tuple(sums)

            sums = tuple(jnp.zeros((B, lanes), jnp.float32) for _ in range(3 * B))
            if total <= 8:
                for t in range(total):
                    sums = add_frame(t, sums)
            else:
                sums = lax.fori_loop(0, total, add_frame, sums)
            sums = [sums[a] - sums[2 * B + a] for a in range(B)] + [sums[a] - sums[B + a] for a in range(B)]
            rows = jnp.concatenate(sums, axis=0) * scale
            out_ref[index, cols, :] = rows.T
        return carry
    lax.fori_loop(0, group, one_tile, 0, unroll=True)


def correlate(gathered, pairs):
    blocks, depth, span = gathered.shape
    total = depth // (2 * B)
    rows = pairs.shape[0]
    group = max(size for size in range(1, 12) if rows % size == 0)
    return pl.pallas_call(
        functools.partial(correlate_kernel, group, 1.0 / total),
        grid_spec=pltpu.PrefetchScalarGridSpec(
            num_scalar_prefetch=1,
            grid=(rows // group,),
            in_specs=[pl.BlockSpec(gathered.shape, lambda i, pairs: (0, 0, 0))],
            out_specs=pl.BlockSpec((group, span, 2 * B * B), lambda i, pairs: (i, 0, 0)),
            scratch_shapes=[pltpu.VMEM((blocks, 4, total, B, span), jnp.float32)],
        ),
        out_shape=jax.ShapeDtypeStruct((rows, span, 2 * B * B), jnp.float32),
        compiler_params=pltpu.CompilerParams(vmem_limit_bytes=48 * 2**20),
        cost_estimate=pl.CostEstimate(
            flops=rows * span * 2 * B * B * 4 * total,
            bytes_accessed=rows * span * 2 * B * B * 4,
            transcendentals=0,
        ),
        name="correlate",
    )(pairs, gathered)


def front_kernel(volts_hbm, gains_hbm, table_hbm, buf, volts_ref, gains_ref, table, outbox, inbox, half, spec,
                 fetch_sem, turn_send, turn_recv, ct_send, ct_recv,
                 up_send, up_recv, down_send, down_recv, core_send, core_recv):
    shards, tiles = lax.axis_size("ct"), lax.axis_size("tile")
    levels = tiles // 2
    taps, channels = gains_hbm.shape
    span = channels // shards
    c, t = lax.axis_index("ct"), lax.axis_index("tile")
    z, k = t // 2, t % 2

    fetch_volts = pltpu.make_async_copy(volts_hbm, volts_ref, fetch_sem.at[0])
    fetch_gains = pltpu.make_async_copy(gains_hbm, gains_ref, fetch_sem.at[1])
    fetch_table = pltpu.make_async_copy(table_hbm, table, fetch_sem.at[2])
    for fetch in (fetch_volts, fetch_gains, fetch_table):
        fetch.start()
    barrier = pltpu.get_barrier_semaphore()
    for off in range(1, tiles):
        pl.semaphore_signal(barrier, inc=1, device_id={"tile": lax.rem(t + off, tiles)}, device_id_type=MESH)
    for off in range(1, shards):
        pl.semaphore_signal(barrier, inc=1, device_id={"ct": lax.rem(c + off, shards)}, device_id_type=MESH)
    fetch_volts.wait()
    for dest in range(tiles):
        part = volts_ref[dest * B:(dest + 1) * B].astype(jnp.float32)
        outbox[dest] = jnp.concatenate([part[:, :channels], part[:, channels:]], axis=0).astype(jnp.bfloat16)
    pl.semaphore_wait(barrier, tiles + shards - 2)

    def turn(off, slot):
        dest = lax.rem(t + off, tiles)
        return pltpu.make_async_remote_copy(
            src_ref=outbox.at[dest], dst_ref=inbox.at[slot],
            send_sem=turn_send.at[off], recv_sem=turn_recv.at[off],
            device_id={"tile": dest}, device_id_type=MESH)

    by_distance = sorted(range(1, tiles), key=lambda off: -min(off, tiles - off))
    for off in by_distance:
        turn(off, t).start()
    inbox[t] = outbox[t]
    for off in range(1, tiles):
        turn(off, lax.rem(t - off + tiles, tiles)).wait_recv()

    fetch_gains.wait()
    for frame in range(tiles):
        total = jnp.zeros((2 * B, channels), jnp.float32)
        for tap in range(min(taps, frame + 1)):
            samples = inbox[frame - tap].astype(jnp.float32) * 0.25
            total = total + gains_ref[tap:tap + 1, :] * samples
        half[frame * 2 * B:(frame + 1) * 2 * B] = total.astype(jnp.bfloat16)
    fetch_table.wait()

    def ct_copy(off, block):
        dest = lax.rem(c + off, shards)
        return pltpu.make_async_remote_copy(
            src_ref=spec.at[dest], dst_ref=buf.at[block, t],
            send_sem=ct_send.at[off], recv_sem=ct_recv.at[off],
            device_id={"ct": dest}, device_id_type=MESH)

    def piece(slab, j, send, recv, dest):
        place = buf.at[lax.rem(c - j + shards, shards), slab]
        return pltpu.make_async_remote_copy(
            src_ref=place, dst_ref=place, send_sem=send, recv_sem=recv,
            device_id={"tile": dest}, device_id_type=MESH)

    def up(d, j):
        return piece(t - 2 * d, j, up_send.at[d, j], up_recv.at[d, j], t + 2)

    def up_arrival(d, j):
        return piece(t - 2 * d, j, up_send.at[d - 1, j], up_recv.at[d - 1, j], t + 2)

    def down(d, j):
        return piece(t + 2 * d, j, down_send.at[d, j], down_recv.at[d, j], t - 2)

    def down_arrival(d, j):
        return piece(t + 2 * d, j, down_send.at[d - 1, j], down_recv.at[d - 1, j], t - 2)

    def core(step, j, other):
        slab = t + 2 * step + (1 - 2 * k if other else 0)
        return piece(slab, j, core_send.at[levels - 1 + step, j], core_recv.at[levels - 1 + step, j], t + 1 - 2 * k)

    def send_own(j):
        @pl.when(z + 1 < levels)
        def _():
            up(0, j).start()

        @pl.when(z >= 1)
        def _():
            down(0, j).start()
        core(0, j, False).start()

    for off in range(shards):
        dest = lax.rem(c + off, shards)
        product = jnp.dot(half[...], table[dest], preferred_element_type=jnp.float32)
        product = product.reshape(tiles, 2, B, 2 * span)
        real = product[:, 0, :, :span] + product[:, 1, :, span:]
        imag = product[:, 1, :, :span] - product[:, 0, :, span:]
        rows = jnp.concatenate([real[:, None], imag[:, None]], axis=1).reshape(tiles * 2 * B, span)
        if off == 0:
            buf[c, t] = rows.astype(jnp.bfloat16)
            send_own(0)
        else:
            spec[dest] = rows.astype(jnp.bfloat16)
            ct_copy(off, c).start()
    for off in range(1, shards):
        ct_copy(off, lax.rem(c - off + shards, shards)).wait_recv()
        send_own(off)

    for d in range(1, levels):
        def pass_on(j, carry, d=d):
            @pl.when(z >= d)
            def _():
                up_arrival(d, j).wait_recv()

                @pl.when(z + 1 < levels)
                def _():
                    up(d, j).start()
                core(-d, j, False).start()

            @pl.when(z + d < levels)
            def _():
                down_arrival(d, j).wait_recv()

                @pl.when(z >= 1)
                def _():
                    down(d, j).start()
                core(d, j, False).start()
            return carry
        lax.fori_loop(0, shards, pass_on, 0)

    for off in range(1, tiles):
        turn(off, t).wait_send()
    for off in range(1, shards):
        ct_copy(off, c).wait_send()
    for d in range(levels):
        def finish(j, carry, d=d):
            @pl.when((z >= d) & (z + 1 < levels))
            def _():
                up(d, j).wait_send()

            @pl.when((z + d < levels) & (z >= 1))
            def _():
                down(d, j).wait_send()

            @pl.when(z >= d)
            def _():
                core(-d, j, False).wait_send()
                core(-d, j, True).wait_recv()
            if d > 0:
                @pl.when(z + d < levels)
                def _():
                    core(d, j, False).wait_send()
                    core(d, j, True).wait_recv()
            return carry
        lax.fori_loop(0, shards, finish, 0)


def front(voltages, fir_taps):
    shards, tiles = lax.axis_size("ct"), lax.axis_size("tile")
    _, in_dev, row_width = voltages.shape
    channels = row_width // 2
    span = channels // shards
    levels = tiles // 2
    table = half_table(channels).reshape(channels, 2, shards, span).transpose(2, 0, 1, 3)
    table = np.ascontiguousarray(table.reshape(shards, channels, 2 * span))
    depth = tiles * 2 * B
    vmem = pl.BlockSpec(memory_space=pltpu.VMEM)
    dma = pltpu.SemaphoreType.DMA
    gathered = pl.pallas_call(
        front_kernel,
        in_specs=[pl.BlockSpec(memory_space=pl.ANY)] * 3,
        out_specs=vmem,
        out_shape=jax.ShapeDtypeStruct((shards, tiles, depth, span), jnp.bfloat16),
        scratch_shapes=[
            pltpu.VMEM((in_dev, row_width), jnp.int32),
            pltpu.VMEM(fir_taps.shape, jnp.float32),
            pltpu.VMEM(table.shape, jnp.bfloat16),
            pltpu.VMEM((tiles, 2 * B, channels), jnp.bfloat16),
            pltpu.VMEM((tiles, 2 * B, channels), jnp.bfloat16),
            pltpu.VMEM((depth, channels), jnp.bfloat16),
            pltpu.VMEM((shards, depth, span), jnp.bfloat16),
            dma((3,)), dma((tiles,)), dma((tiles,)), dma((shards,)), dma((shards,)),
            dma((levels, shards)), dma((levels, shards)), dma((levels, shards)), dma((levels, shards)),
            dma((2 * levels - 1, shards)), dma((2 * levels - 1, shards)),
        ],
        compiler_params=pltpu.CompilerParams(
            collective_id=0, has_side_effects=True, vmem_limit_bytes=48 * 2**20),
        cost_estimate=pl.CostEstimate(
            flops=depth * channels * 4 * channels, bytes_accessed=4 * channels * channels, transcendentals=0),
        name="front",
    )(voltages[0], fir_taps, jnp.asarray(table))
    return gathered.reshape(shards * tiles, depth, span)


def front_by_collectives(voltages, fir_taps):
    frames, in_dev, row_width = voltages.shape
    channels = row_width // 2
    taps = fir_taps.shape[0]
    shards = lax.axis_size("ct")
    span = channels // shards
    volts = voltages.astype(jnp.bfloat16)
    history = jnp.concatenate(earlier_frames(volts, taps - 1) + [volts], axis=0)
    history = history.astype(jnp.float32) * 0.25
    gains = jnp.concatenate([fir_taps, fir_taps], axis=1)
    filtered = jnp.zeros((frames, in_dev, row_width), jnp.float32)
    for tap in range(taps):
        start = taps - 1 - tap
        filtered = filtered + gains[tap][None, None, :] * history[start:start + frames]
    filtered = filtered.astype(jnp.bfloat16)
    halves = jnp.stack([filtered[..., :channels], filtered[..., channels:]], axis=1)
    products = jnp.dot(
        halves.reshape(frames * 2 * in_dev, channels),
        jnp.asarray(half_table(channels)),
        preferred_element_type=jnp.float32,
    ).reshape(frames, 2, in_dev, 2, shards, span)
    real = products[:, 0, :, 0] + products[:, 1, :, 1]
    imag = products[:, 1, :, 0] - products[:, 0, :, 1]
    spectra = jnp.stack([real, imag], axis=1).astype(jnp.bfloat16)
    spectra = spectra.transpose(3, 0, 1, 2, 4)
    turned = lax.all_to_all(spectra, "ct", split_axis=0, concat_axis=0, tiled=True)
    gathered = lax.all_gather(turned, "tile", axis=0, tiled=False)
    tiles = gathered.shape[0]
    gathered = gathered.reshape(tiles, shards, frames, 2, in_dev // B, B, span).transpose(1, 4, 0, 2, 3, 5, 6)
    return gathered.reshape(shards * in_dev // B, tiles * frames * 2 * B, span)


def per_device(voltages, fir_taps, tile_map):
    frames, in_dev, _ = voltages.shape
    tiles = lax.axis_size("tile")
    one_block_each = frames == 1 and in_dev == tiles * B and tiles % 2 == 0
    make = front if one_block_each else front_by_collectives
    return correlate(make(voltages, fir_taps), tile_map)


def solution(mesh):
    in_specs = (P("tile", "ct", None), P(), P("tile", None))
    out_specs = P("tile", "ct", None)
    return jax.shard_map(
        per_device, mesh=mesh, in_specs=in_specs, out_specs=out_specs, check_vma=False
    )
```
